512 devices in a mesh: dp: 32 (over y, x_hi, core), mp: 16 (over x_lo, z).
Axes of the slice: x: 4 (x_hi: 2, x_lo: 2; x = x_hi * 2 + x_lo), y: 8, z: 8, core: 2. Of those that a mesh axis runs over, the one named last changes fastest.
Arguments:
- activations: bfloat16 [16384, 4096], P('dp'), may hold values from -6 to 6
- out_grads: bfloat16 [16384, 4096], P('dp', 'mp'), may hold values from -0.046875 to 0.046875
- input_inverse: bfloat16 [4096, 256], P('mp'), may hold values from -0.09375 to 2
- output_inverse: bfloat16 [4096, 256], P('mp'), may hold values from -0.09375 to 2
Outputs:
- preconditioned: bfloat16 [4096, 4096], P('mp', 'dp')
The draws below stay inside these ranges and needn't reach their ends.
All inputs are finite; a program needn't handle non-finite values.
Results may differ from the reference program's by a relative error of at most 0.0058.
Values may be sent and summed in bfloat16 or wider, within the bound.
No kernel may reach another device: no remote copies, remote signals or barrier semaphores. Data moves between devices by JAX's collectives and lax.ppermute only.
A program may use at most 64 MiB of HBM per device.

```python
import math
import jax
import jax.numpy as jnp
from jax import lax

DIN = 4096
DOUT = 4096
BLK = 256
TOKENS = 16384


def factor_blocks(key, row_count, low_diag, high_diag):
    first_key, second_key = jax.random.split(key)
    spread = jax.random.uniform(first_key, (row_count, BLK), jnp.float32, -0.09375, 0.09375)
    diag_vals = jnp.exp(jax.random.uniform(second_key, (row_count, 1), jnp.float32, math.log(low_diag), math.log(high_diag)))
    diag_vals = jnp.clip(diag_vals, low_diag, high_diag)
    on_diag = (jnp.arange(row_count) % BLK)[:, None] == jnp.arange(BLK)[None, :]
    return jnp.where(on_diag, diag_vals, spread).astype(jnp.bfloat16)


def draw_input_inverse(key, part):
    key = jax.random.fold_in(key, 17)
    return factor_blocks(key, DIN, 0.5, 2.0)


def draw_output_inverse(key, part):
    key = jax.random.fold_in(key, 29)
    return factor_blocks(key, DOUT, 0.5, 2.0)


def shard_levels(key, dims, cuts, low, high):
    loudness, own = 1.0, jax.random.fold_in(key, 6)
    for dim, shards_of in cuts:
        steps = jnp.exp(jax.random.uniform(jax.random.fold_in(own, dim), (shards_of,), jnp.float32, low / len(cuts), high / len(cuts)))
        loudness = loudness * jnp.repeat(steps, dims[dim] // shards_of).reshape([-1 if axis == dim else 1 for axis in range(len(dims))])
    return loudness


def bell_draw(rng, dims, deviation, bound, pieces=(), kind=jnp.bfloat16):
    values = jax.random.normal(rng, dims, jnp.float32) * deviation
    if len(pieces) > 0:
        values = shard_levels(rng, dims, pieces, -0.22, 0.18) * values
    return jnp.clip(values, min=-bound, max=bound).astype(kind)


def setup_inputs(seed: int = 0) -> dict:
    splits = jax.random.split(jax.random.key(seed), 5)
    activations = bell_draw(splits[0], (TOKENS, DIN), 1.0, 6.0, ((0, 32),))
    out_grads = bell_draw(splits[1], (TOKENS, DOUT), TOKENS ** -0.5, 0.046875, ((0, 32), (1, 16)))
    input_inverse = draw_input_inverse(jax.random.fold_in(splits[4], 71), 0)
    output_inverse = draw_output_inverse(jax.random.fold_in(splits[4], 71), 0)
    return {"activations": activations, "out_grads": out_grads, "input_inverse": input_inverse, "output_inverse": output_inverse}


def reference(activations, out_grads, input_inverse, output_inverse):
    grad_full = lax.dot_general(out_grads.astype(jnp.float32), activations.astype(jnp.float32), (((0,), (0,)), ((), ())), precision=lax.Precision.HIGHEST)
    gradient = grad_full.astype(jnp.bfloat16)
    in_blocks = DIN // BLK
    out_blocks = DOUT // BLK
    righted = jnp.einsum("oik,ikc->oic", gradient.astype(jnp.float32).reshape(DOUT, in_blocks, BLK), input_inverse.astype(jnp.float32).reshape(in_blocks, BLK, BLK), precision=lax.Precision.HIGHEST)
    righted = righted.astype(jnp.bfloat16).reshape(DOUT, DIN)
    result = jnp.einsum("jrk,jkc->jrc", output_inverse.astype(jnp.float32).reshape(out_blocks, BLK, BLK), righted.astype(jnp.float32).reshape(out_blocks, BLK, DIN), precision=lax.Precision.HIGHEST)
    return result.astype(jnp.bfloat16).reshape(DOUT, DIN)
```

```python
import functools

import jax
import jax.numpy as jnp
from jax import lax
from jax.experimental import pallas as pl
from jax.experimental.pallas import tpu as pltpu
from jax.sharding import Mesh, PartitionSpec as P

F32, BF16 = jnp.float32, jnp.bfloat16
AXES = ("y", "xh", "core", "mp")


def pairs(shape, move):
    y_n, x_n, c_n, m_n = shape

    def flat(y, x, c, m):
        return ((y * x_n + x) * c_n + c) * m_n + m

    return [
        (flat(y, x, c, m), flat(*move(y, x, c, m)))
        for y in range(y_n)
        for x in range(x_n)
        for c in range(c_n)
        for m in range(m_n)
    ]


def partial_kernel(core_ref, grads_ref, left_ref, act_ref, send_ref, keep_ref, turned):
    half, x_n = send_ref.shape[2], send_ref.shape[0]
    width = send_ref.shape[3]

    @pl.when(pl.program_id(0) == 0)
    def _():
        for part in range(2):
            first = pl.multiple_of((core_ref[0] ^ (1 - part)) * half, half)
            turned[part * half : (part + 1) * half] = lax.dot_general(
                left_ref[pl.ds(first, half)],
                grads_ref[...],
                (((1,), (1,)), ((), ())),
                preferred_element_type=F32,
            ).astype(BF16)

    product = jnp.dot(turned[...], act_ref[...], preferred_element_type=F32)
    for x in range(x_n):
        columns = slice(x * width, (x + 1) * width)
        send_ref[x, 0] = product[:half, columns].astype(BF16)
        keep_ref[x, 0] = product[half:, columns]


def partials(shape, core, activations, out_grads, output_inverse):
    y_n, x_n, c_n, _ = shape
    tokens, features = activations.shape
    rows = out_grads.shape[1]
    half, width = rows // c_n, features // (y_n * x_n)
    blocks = (x_n, y_n, half, width)
    piece = pl.BlockSpec((x_n, 1, half, width), lambda y: (0, y, 0, 0))
    return pl.pallas_call(
        partial_kernel,
        grid=(y_n,),
        out_shape=(jax.ShapeDtypeStruct(blocks, BF16), jax.ShapeDtypeStruct(blocks, F32)),
        in_specs=[
            pl.BlockSpec(memory_space=pltpu.SMEM),
            pl.BlockSpec((tokens, rows), lambda y: (0, 0)),
            pl.BlockSpec((rows, rows), lambda y: (0, 0)),
            pl.BlockSpec((tokens, x_n * width), lambda y: (0, y)),
        ],
        out_specs=(piece, piece),
        scratch_shapes=[pltpu.VMEM((rows, tokens), BF16)],
        compiler_params=pltpu.CompilerParams(vmem_limit_bytes=16 * 2**20),
    )(core.reshape(1), out_grads, output_inverse, activations)


def right_kernel(core_ref, pieces_ref, block_ref, send_ref, own_ref):
    total = pieces_ref[0].astype(F32)
    for y in range(1, pieces_ref.shape[0]):
        total += pieces_ref[y].astype(F32)
    narrow = send_ref.shape[1]
    total = total.astype(BF16)
    for ref, core in ((send_ref, 1 - core_ref[0]), (own_ref, core_ref[0])):
        first = pl.multiple_of(core * narrow, narrow)
        ref[...] = jnp.dot(
            total, block_ref[:, pl.ds(first, narrow)], preferred_element_type=F32
        ).astype(BF16)


def right(core, pieces, block):
    _, half, width = pieces.shape
    part = jax.ShapeDtypeStruct((half, width // 2), BF16)
    vmem = pl.BlockSpec(memory_space=pltpu.VMEM)
    return pl.pallas_call(
        right_kernel,
        out_shape=(part, part),
        in_specs=[pl.BlockSpec(memory_space=pltpu.SMEM), vmem, vmem],
        out_specs=(vmem, vmem),
    )(core.reshape(1), pieces, block)


def per_device(shape, activations, out_grads, input_inverse, output_inverse):
    core, xh = lax.axis_index("core"), lax.axis_index("xh")
    x_n = shape[1]

    def to_core(a):
        return lax.ppermute(a, AXES, pairs(shape, lambda y, x, c, m: (y, x, 1 - c, m)))

    def to_x(a):
        return lax.ppermute(a, AXES, pairs(shape, lambda y, x, c, m: (y, 1 - x, c, m)))

    def transpose(y, x, c, m):
        return (m // x_n, m % x_n, c, y * x_n + x)

    block = lax.ppermute(input_inverse, AXES, pairs(shape, transpose))
    send, keep = partials(shape, core, activations, out_grads, output_inverse)
    got = to_core(send)

    def summed(x):
        return lax.dynamic_index_in_dim(keep, x, 0, keepdims=False) + lax.dynamic_index_in_dim(
            got, x, 0, keepdims=False
        ).astype(F32)

    total = (summed(xh) + to_x(summed(1 - xh).astype(BF16)).astype(F32)).astype(BF16)
    pieces = lax.all_to_all(total, "y", 0, 0)
    send, own = right(core, pieces, block)
    other = to_core(send)
    return jnp.where(
        core == 0, jnp.concatenate([own, other], 0), jnp.concatenate([other, own], 0)
    )


def solution(mesh):
    dp_count, mp_count = mesh.devices.shape
    shape = (dp_count // 4, 2, 2, mp_count)
    split = Mesh(mesh.devices.reshape(shape), AXES)
    dp = AXES[:3]
    in_specs = (P(dp, None), P(dp, "mp"), P("mp", None), P("mp", None))
    return jax.shard_map(
        functools.partial(per_device, shape),
        mesh=split,
        in_specs=in_specs,
        out_specs=P("mp", dp),
        check_vma=False,
    )
```

```python
import functools

import jax
import jax.numpy as jnp
from jax import lax
from jax.experimental import pallas as pl
from jax.experimental.pallas import tpu as pltpu
from jax.sharding import Mesh, PartitionSpec as P

F32, BF16 = jnp.float32, jnp.bfloat16
AXES = ("y", "xh", "core", "mp")
VMEM = pl.BlockSpec(memory_space=pltpu.VMEM)
SMEM = pl.BlockSpec(memory_space=pltpu.SMEM)


def pairs(shape, move):
    y_n, x_n, c_n, m_n = shape

    def flat(y, x, c, m):
        return ((y * x_n + x) * c_n + c) * m_n + m

    return [
        (flat(y, x, c, m), flat(*move(y, x, c, m)))
        for y in range(y_n)
        for x in range(x_n)
        for c in range(c_n)
        for m in range(m_n)
    ]


def spread(shape):
    y_n, x_n, _, m_n = shape
    z_n = m_n // 2

    def move(y, x, c, m):
        to_y, to_x = m // x_n, m % x_n
        low = (m // z_n) ^ x ^ to_x
        return to_y, to_x, c, low * z_n + (m % z_n + y - to_y + z_n // 2) % z_n

    return pairs(shape, move)


def partial_kernel(core_ref, grads_hbm, left_hbm, act_hbm, send_ref, keep_ref, grads, left, act, turned, sems):
    _, half, width = send_ref.shape
    tiles, _, columns = act.shape
    copies = [
        pltpu.make_async_copy(grads_hbm, grads, sems.at[0]),
        pltpu.make_async_copy(left_hbm, left, sems.at[1]),
    ]
    for tile in range(tiles):
        source = act_hbm.at[:, pl.ds(tile * columns, columns)]
        copies.append(pltpu.make_async_copy(source, act.at[tile], sems.at[2 + tile]))
    for copy in copies:
        copy.start()
    copies[0].wait()
    copies[1].wait()
    for part in range(2):
        first = pl.multiple_of((core_ref[0] ^ (1 - part)) * half, half)
        turned[part * half : (part + 1) * half] = lax.dot_general(
            left[pl.ds(first, half)],
            grads[...],
            (((1,), (1,)), ((), ())),
            preferred_element_type=F32,
        ).astype(BF16)
    for tile in range(tiles):
        copies[2 + tile].wait()
        product = jnp.dot(turned[...], act[tile], preferred_element_type=F32)
        for part in range(columns // width):
            piece = tile * (columns // width) + part
            block = product[:, part * width : (part + 1) * width]
            send_ref[piece] = block[:half].astype(BF16)
            keep_ref[piece] = block[half:]


def partials(shape, core, activations, out_grads, output_inverse, tiles=4):
    y_n, x_n, c_n, _ = shape
    tokens, features = activations.shape
    rows = out_grads.shape[1]
    blocks = (y_n * x_n, rows // c_n, features // (y_n * x_n))
    hbm = pl.BlockSpec(memory_space=pl.ANY)
    return pl.pallas_call(
        partial_kernel,
        out_shape=(pltpu.VMEM(blocks, BF16), pltpu.VMEM(blocks, F32)),
        in_specs=[SMEM, hbm, hbm, hbm],
        out_specs=(VMEM, VMEM),
        scratch_shapes=[
            pltpu.VMEM(out_grads.shape, BF16),
            pltpu.VMEM(output_inverse.shape, BF16),
            pltpu.VMEM((tiles, tokens, features // tiles), BF16),
            pltpu.VMEM((rows, tokens), BF16),
            pltpu.SemaphoreType.DMA((2 + tiles,)),
        ],
        compiler_params=pltpu.CompilerParams(vmem_limit_bytes=54 * 2**20),
    )(core.reshape(1), out_grads, output_inverse, activations)


def add_kernel(keep_ref, got_ref, total_ref):
    for piece in range(keep_ref.shape[0]):
        total_ref[piece] = (keep_ref[piece] + got_ref[piece].astype(F32)).astype(BF16)


def add(keep, got):
    return pl.pallas_call(
        add_kernel,
        out_shape=jax.ShapeDtypeStruct(got.shape, BF16),
        in_specs=[VMEM, VMEM],
        out_specs=VMEM,
        compiler_params=pltpu.CompilerParams(vmem_limit_bytes=16 * 2**20),
    )(keep, got)


def sum_kernel(pieces_ref, total_ref):
    total = pieces_ref[0].astype(F32)
    for piece in range(1, pieces_ref.shape[0]):
        total += pieces_ref[piece].astype(F32)
    total_ref[...] = total.astype(BF16)


def sum_pieces(pieces):
    return pl.pallas_call(
        sum_kernel,
        out_shape=jax.ShapeDtypeStruct(pieces.shape[1:], BF16),
        in_specs=[VMEM],
        out_specs=VMEM,
        compiler_params=pltpu.CompilerParams(vmem_limit_bytes=8 * 2**20),
    )(pieces)


def right_kernel(core_ref, own_ref, other_ref, block_ref, out_ref):
    half = own_ref.shape[0]
    core = core_ref[0]
    for ref, index in ((own_ref, core), (other_ref, 1 - core)):
        first = pl.multiple_of(index * half, half)
        out_ref[pl.ds(first, half)] = jnp.dot(
            ref[...], block_ref[...], preferred_element_type=F32
        ).astype(BF16)


def right(core, own, other, block):
    half, width = own.shape
    return pl.pallas_call(
        right_kernel,
        out_shape=jax.ShapeDtypeStruct((2 * half, width // 2), BF16),
        in_specs=[SMEM, VMEM, VMEM, VMEM],
        out_specs=VMEM,
        compiler_params=pltpu.CompilerParams(vmem_limit_bytes=8 * 2**20),
    )(core.reshape(1), own, other, block)


def per_device(shape, activations, out_grads, input_inverse, output_inverse):
    core = lax.axis_index("core")

    def to_core(a):
        return lax.ppermute(a, AXES, pairs(shape, lambda y, x, c, m: (y, x, 1 - c, m)))

    narrow = input_inverse.shape[1] // 2
    block = lax.dynamic_slice_in_dim(input_inverse, core * narrow, narrow, 1)
    block = lax.ppermute(block, AXES, spread(shape))
    send, keep = partials(shape, core, activations, out_grads, output_inverse)
    total = add(keep, to_core(send))
    gathered = sum_pieces(lax.all_to_all(total, ("y", "xh"), 0, 0))
    return right(core, gathered, to_core(gathered), block)


def solution(mesh):
    dp_count, mp_count = mesh.devices.shape
    shape = (dp_count // 4, 2, 2, mp_count)
    split = Mesh(mesh.devices.reshape(shape), AXES)
    dp = AXES[:3]
    in_specs = (P(dp, None), P(dp, "mp"), P("mp", None), P("mp", None))
    return jax.shard_map(
        functools.partial(per_device, shape),
        mesh=split,
        in_specs=in_specs,
        out_specs=P("mp", dp),
        check_vma=False,
    )
```

```python
import functools

import jax
import jax.numpy as jnp
from jax import lax
from jax.experimental import pallas as pl
from jax.experimental.pallas import tpu as pltpu
from jax.sharding import Mesh, PartitionSpec as P

F32, BF16 = jnp.float32, jnp.bfloat16
AXES = ("y", "xh", "core", "mp")
VMEM = pl.BlockSpec(memory_space=pltpu.VMEM)
SMEM = pl.BlockSpec(memory_space=pltpu.SMEM)


def pairs(shape, move):
    y_n, x_n, c_n, m_n = shape

    def flat(y, x, c, m):
        return ((y * x_n + x) * c_n + c) * m_n + m

    return [
        (flat(y, x, c, m), flat(*move(y, x, c, m)))
        for y in range(y_n)
        for x in range(x_n)
        for c in range(c_n)
        for m in range(m_n)
    ]


def spread(shape):
    y_n, x_n, _, m_n = shape
    z_n = m_n // 2

    def move(y, x, c, m):
        to_y, to_x = m // x_n, m % x_n
        low = (m // z_n) ^ x ^ to_x
        return to_y, to_x, c, low * z_n + (m % z_n + y - to_y + z_n // 2) % z_n

    whole = pairs(shape, move)
    down = [(a, b) for a, b in whole if b % z_n <= a % z_n]
    return down, [pair for pair in whole if pair not in down]


def partial_kernel(
    core_ref, grads_hbm, left_hbm, right_hbm, act_hbm, send_ref, keep_ref, half_ref, grads, left, act, turned, sems
):
    _, half, width = send_ref.shape
    tiles, _, columns = act.shape
    copies = [
        pltpu.make_async_copy(grads_hbm, grads, sems.at[0]),
        pltpu.make_async_copy(left_hbm, left, sems.at[1]),
    ]
    for tile in range(tiles):
        source = act_hbm.at[:, pl.ds(tile * columns, columns)]
        copies.append(pltpu.make_async_copy(source, act.at[tile], sems.at[2 + tile]))
    narrow = half_ref.shape[1]
    source = right_hbm.at[:, pl.ds(pl.multiple_of(core_ref[0] * narrow, narrow), narrow)]
    copies.append(pltpu.make_async_copy(source, half_ref, sems.at[2 + tiles]))
    for copy in copies:
        copy.start()
    copies[0].wait()
    copies[1].wait()
    for part in range(2):
        first = pl.multiple_of((core_ref[0] ^ (1 - part)) * half, half)
        turned[part * half : (part + 1) * half] = lax.dot_general(
            left[pl.ds(first, half)],
            grads[...],
            (((1,), (1,)), ((), ())),
            preferred_element_type=F32,
        ).astype(BF16)
    for tile in range(tiles):
        copies[2 + tile].wait()
        product = jnp.dot(turned[...], act[tile], preferred_element_type=F32)
        for part in range(columns // width):
            piece = tile * (columns // width) + part
            block = product[:, part * width : (part + 1) * width]
            send_ref[piece] = block[:half].astype(BF16)
            keep_ref[piece] = block[half:]
    copies[-1].wait()


def partials(shape, core, activations, out_grads, input_inverse, output_inverse, tiles=4):
    y_n, x_n, c_n, _ = shape
    tokens, features = activations.shape
    rows = out_grads.shape[1]
    half = (input_inverse.shape[0], input_inverse.shape[1] // c_n)
    blocks = (y_n * x_n, rows // c_n, features // (y_n * x_n))
    hbm = pl.BlockSpec(memory_space=pl.ANY)
    return pl.pallas_call(
        partial_kernel,
        out_shape=(pltpu.VMEM(blocks, BF16), pltpu.VMEM(blocks, F32), pltpu.VMEM(half, BF16)),
        in_specs=[SMEM, hbm, hbm, hbm, hbm],
        out_specs=(VMEM, VMEM, VMEM),
        scratch_shapes=[
            pltpu.VMEM(out_grads.shape, BF16),
            pltpu.VMEM(output_inverse.shape, BF16),
            pltpu.VMEM((tiles, tokens, features // tiles), BF16),
            pltpu.VMEM((rows, tokens), BF16),
            pltpu.SemaphoreType.DMA((3 + tiles,)),
        ],
        compiler_params=pltpu.CompilerParams(vmem_limit_bytes=54 * 2**20),
    )(core.reshape(1), out_grads, output_inverse, input_inverse, activations)


def add_kernel(keep_ref, got_ref, total_ref):
    for piece in range(keep_ref.shape[0]):
        total_ref[piece] = (keep_ref[piece] + got_ref[piece].astype(F32)).astype(BF16)


def add(keep, got):
    return pl.pallas_call(
        add_kernel,
        out_shape=jax.ShapeDtypeStruct(got.shape, BF16),
        in_specs=[VMEM, VMEM],
        out_specs=VMEM,
        compiler_params=pltpu.CompilerParams(vmem_limit_bytes=16 * 2**20),
    )(keep, got)


def sum_kernel(pieces_ref, _, total_ref):
    total = pieces_ref[0].astype(F32)
    for piece in range(1, pieces_ref.shape[0]):
        total += pieces_ref[piece].astype(F32)
    total_ref[...] = total.astype(BF16)


def sum_pieces(pieces, first):
    return pl.pallas_call(
        sum_kernel,
        out_shape=jax.ShapeDtypeStruct(pieces.shape[1:], BF16),
        in_specs=[VMEM, VMEM],
        out_specs=VMEM,
        compiler_params=pltpu.CompilerParams(vmem_limit_bytes=8 * 2**20),
    )(pieces, first)


def right_kernel(core_ref, own_ref, other_ref, near_ref, far_ref, out_ref):
    half = own_ref.shape[0]
    core = core_ref[0]
    block = near_ref[...] + far_ref[...]
    for ref, index in ((own_ref, core), (other_ref, 1 - core)):
        first = pl.multiple_of(index * half, half)
        out_ref[pl.ds(first, half)] = jnp.dot(
            ref[...], block, preferred_element_type=F32
        ).astype(BF16)


def right(core, own, other, near, far):
    half, width = own.shape
    return pl.pallas_call(
        right_kernel,
        out_shape=jax.ShapeDtypeStruct((2 * half, width // 2), BF16),
        in_specs=[SMEM, VMEM, VMEM, VMEM, VMEM],
        out_specs=VMEM,
        compiler_params=pltpu.CompilerParams(vmem_limit_bytes=8 * 2**20),
    )(core.reshape(1), own, other, near, far)


def hold_kernel(block_ref, out_ref):
    out_ref[...] = block_ref[...]


def hold(block):
    return pl.pallas_call(
        hold_kernel,
        out_shape=jax.ShapeDtypeStruct(block.shape, BF16),
        in_specs=[VMEM],
        out_specs=VMEM,
        compiler_params=pltpu.CompilerParams(vmem_limit_bytes=4 * 2**20),
        cost_estimate=pl.CostEstimate(flops=5 * 10**10, bytes_accessed=2**17, transcendentals=0),
    )(block)


def per_device(shape, activations, out_grads, input_inverse, output_inverse):
    core = lax.axis_index("core")

    def to_core(a):
        return lax.ppermute(a, AXES, pairs(shape, lambda y, x, c, m: (y, x, 1 - c, m)))

    send, keep, half = partials(shape, core, activations, out_grads, input_inverse, output_inverse)
    down, up = spread(shape)
    near = lax.ppermute(half, AXES, down)
    total = add(keep, to_core(send))
    total, half = lax.optimization_barrier((total, half))
    far = lax.ppermute(half, AXES, up)
    pieces = lax.all_to_all(total, ("y", "xh"), 0, 0)
    near = hold(near)
    gathered = sum_pieces(pieces, near)
    return right(core, gathered, to_core(gathered), near, far)


def solution(mesh):
    dp_count, mp_count = mesh.devices.shape
    shape = (dp_count // 4, 2, 2, mp_count)
    split = Mesh(mesh.devices.reshape(shape), AXES)
    dp = AXES[:3]
    in_specs = (P(dp, None), P(dp, "mp"), P("mp", None), P("mp", None))
    return jax.shard_map(
        functools.partial(per_device, shape),
        mesh=split,
        in_specs=in_specs,
        out_specs=P("mp", dp),
        check_vma=False,
    )
```

```python
import functools

import jax
import jax.numpy as jnp
from jax import lax
from jax.experimental import pallas as pl
from jax.experimental.pallas import tpu as pltpu
from jax.sharding import Mesh, PartitionSpec as P

F32, BF16 = jnp.float32, jnp.bfloat16
AXES = ("yk", "yp", "xh", "core", "mp")
VMEM = pl.BlockSpec(memory_space=pltpu.VMEM)
SMEM = pl.BlockSpec(memory_space=pltpu.SMEM)


def pairs(shape, move):
    y_n, x_n, c_n, m_n = shape

    def flat(y, x, c, m):
        return ((y * x_n + x) * c_n + c) * m_n + m

    return [
        (flat(y, x, c, m), flat(*move(y, x, c, m)))
        for y in range(y_n)
        for x in range(x_n)
        for c in range(c_n)
        for m in range(m_n)
    ]


def spread(shape):
    y_n, x_n, _, m_n = shape
    z_n = m_n // 2

    def move(y, x, c, m):
        to_y, to_x = m // x_n, m % x_n
        low = (m // z_n) ^ x ^ to_x
        return to_y, to_x, c, low * z_n + (m % z_n + 3 * (y - to_y) + c * (z_n // 2)) % z_n

    whole = pairs(shape, move)
    down = [(a, b) for a, b in whole if b % z_n < a % z_n]
    return down, [pair for pair in whole if pair not in down]


def partial_kernel(
    core_ref, grads_hbm, left_hbm, right_hbm, act_hbm, send_hbm, keep_ref, half_ref, grads, left, act, turned, send, sems, send_sems
):
    _, half, width = send.shape
    tiles, _, columns = act.shape
    copies = [
        pltpu.make_async_copy(grads_hbm, grads, sems.at[0]),
        pltpu.make_async_copy(left_hbm, left, sems.at[1]),
    ]
    for tile in range(tiles):
        source = act_hbm.at[:, pl.ds(tile * columns, columns)]
        copies.append(pltpu.make_async_copy(source, act.at[tile], sems.at[2 + tile]))
    narrow = half_ref.shape[1]
    source = right_hbm.at[:, pl.ds(pl.multiple_of(core_ref[0] * narrow, narrow), narrow)]
    copies.append(pltpu.make_async_copy(source, half_ref, sems.at[2 + tiles]))
    for copy in copies:
        copy.start()
    copies[0].wait()
    copies[1].wait()
    for part in range(2):
        first = pl.multiple_of((core_ref[0] ^ (1 - part)) * half, half)
        turned[part * half : (part + 1) * half] = lax.dot_general(
            left[pl.ds(first, half)],
            grads[...],
            (((1,), (1,)), ((), ())),
            preferred_element_type=F32,
        ).astype(BF16)
    for tile in range(tiles):
        copies[2 + tile].wait()
        product = jnp.dot(turned[...], act[tile], preferred_element_type=F32)
        for part in range(columns // width):
            piece = tile * (columns // width) + part
            block = product[:, part * width : (part + 1) * width]
            send[piece] = block[:half].astype(BF16)
            keep_ref[piece] = block[half:]
        part = pl.ds(tile * (columns // width), columns // width)
        out = pltpu.make_async_copy(send.at[part], send_hbm.at[part], send_sems.at[tile])
        out.start()
        copies.append(out)
    for copy in copies[2 + tiles :]:
        copy.wait()


def partials(shape, core, activations, out_grads, input_inverse, output_inverse, tiles=4):
    y_n, x_n, c_n, _ = shape
    tokens, features = activations.shape
    rows = out_grads.shape[1]
    half = (input_inverse.shape[0], input_inverse.shape[1] // c_n)
    blocks = (y_n * x_n, rows // c_n, features // (y_n * x_n))
    hbm = pl.BlockSpec(memory_space=pl.ANY)
    operands = out_grads, output_inverse, input_inverse, activations
    operands = [pltpu.with_memory_space_constraint(a, pltpu.HBM) for a in operands]
    return pl.pallas_call(
        partial_kernel,
        out_shape=(pltpu.HBM(blocks, BF16), pltpu.VMEM(blocks, F32), pltpu.VMEM(half, BF16)),
        in_specs=[SMEM, hbm, hbm, hbm, hbm],
        out_specs=(hbm, VMEM, VMEM),
        scratch_shapes=[
            pltpu.VMEM(out_grads.shape, BF16),
            pltpu.VMEM(output_inverse.shape, BF16),
            pltpu.VMEM((tiles, tokens, features // tiles), BF16),
            pltpu.VMEM((rows, tokens), BF16),
            pltpu.VMEM(blocks, BF16),
            pltpu.SemaphoreType.DMA((3 + tiles,)),
            pltpu.SemaphoreType.DMA((tiles,)),
        ],
        compiler_params=pltpu.CompilerParams(vmem_limit_bytes=16 * 2**20),
    )(core.reshape(1), *operands)


def pieces_of(parity, count):
    return [4 * (block // 2) + 2 * parity + block % 2 for block in range(count)]


def first_kernel(parity_ref, keep_ref, got_ref, send_ref, rest_ref):
    parity = parity_ref[0]
    count = send_ref.shape[0]
    for block, piece in enumerate(pieces_of(1 - parity, count)):
        send_ref[block] = (keep_ref[piece] + got_ref[piece].astype(F32)).astype(BF16)
    for block, piece in enumerate(pieces_of(parity, count)):
        rest_ref[block] = keep_ref[piece] + got_ref[piece].astype(F32)


def first_sum(parity, keep, got):
    count, half, width = got.shape
    shape = (count // 2, half, width)
    return pl.pallas_call(
        first_kernel,
        out_shape=(pltpu.VMEM(shape, BF16), pltpu.VMEM(shape, F32)),
        in_specs=[SMEM, VMEM, VMEM],
        out_specs=(VMEM, VMEM),
        compiler_params=pltpu.CompilerParams(vmem_limit_bytes=8 * 2**20),
    )(parity.reshape(1), keep, got)


def second_kernel(rest_ref, got_ref, total_hbm, total_ref, sems):
    copies = []
    for block in range(rest_ref.shape[0]):
        total_ref[block] = (rest_ref[block] + got_ref[block].astype(F32)).astype(BF16)
        if block % 2:
            pair = pl.ds(block - 1, 2)
            copies.append(pltpu.make_async_copy(total_ref.at[pair], total_hbm.at[pair], sems.at[block // 2]))
            copies[-1].start()
    for copy in copies:
        copy.wait()


def second_sum(rest, got):
    return pl.pallas_call(
        second_kernel,
        out_shape=pltpu.HBM(got.shape, BF16),
        in_specs=[VMEM, VMEM],
        out_specs=pl.BlockSpec(memory_space=pl.ANY),
        scratch_shapes=[pltpu.VMEM(got.shape, BF16), pltpu.SemaphoreType.DMA((got.shape[0] // 2,))],
        compiler_params=pltpu.CompilerParams(vmem_limit_bytes=8 * 2**20),
    )(rest, got)


def sum_kernel(pieces_ref, _, total_ref):
    total = pieces_ref[0].astype(F32)
    for piece in range(1, pieces_ref.shape[0]):
        total += pieces_ref[piece].astype(F32)
    total_ref[...] = total.astype(BF16)


def sum_pieces(pieces, held):
    return pl.pallas_call(
        sum_kernel,
        out_shape=jax.ShapeDtypeStruct(pieces.shape[1:], BF16),
        in_specs=[VMEM, VMEM],
        out_specs=VMEM,
        compiler_params=pltpu.CompilerParams(vmem_limit_bytes=8 * 2**20),
    )(pieces, held)


def right_kernel(core_ref, own_ref, other_ref, near_ref, far_ref, out_ref):
    half = own_ref.shape[0]
    core = core_ref[0]
    block = near_ref[...] + far_ref[...]
    for ref, index in ((own_ref, core), (other_ref, 1 - core)):
        first = pl.multiple_of(index * half, half)
        out_ref[pl.ds(first, half)] = jnp.dot(
            ref[...], block, preferred_element_type=F32
        ).astype(BF16)


def right(core, own, other, near, far):
    half, width = own.shape
    return pl.pallas_call(
        right_kernel,
        out_shape=jax.ShapeDtypeStruct((2 * half, width // 2), BF16),
        in_specs=[SMEM, VMEM, VMEM, VMEM, VMEM],
        out_specs=VMEM,
        compiler_params=pltpu.CompilerParams(vmem_limit_bytes=8 * 2**20),
    )(core.reshape(1), own, other, near, far)


def hold_kernel(block_ref, out_ref):
    out_ref[...] = block_ref[...]


def hold(block):
    return pl.pallas_call(
        hold_kernel,
        out_shape=jax.ShapeDtypeStruct(block.shape, BF16),
        in_specs=[VMEM],
        out_specs=VMEM,
        compiler_params=pltpu.CompilerParams(vmem_limit_bytes=4 * 2**20),
        cost_estimate=pl.CostEstimate(flops=5 * 10**10, bytes_accessed=2**17, transcendentals=0),
    )(block)


def per_device(shape, activations, out_grads, input_inverse, output_inverse):
    core, parity = lax.axis_index("core"), lax.axis_index("yp")
    y_n = shape[0]

    def to_core(a):
        return lax.ppermute(a, AXES, pairs(shape, lambda y, x, c, m: (y, x, 1 - c, m)))

    def to_y(a):
        def move(y, x, c, m):
            return (((y + c) % y_n ^ 1) - c) % y_n, x, c, m

        return lax.ppermute(a, AXES, pairs(shape, move))

    send, keep, half = partials(shape, core, activations, out_grads, input_inverse, output_inverse)
    lower, higher = spread(shape)
    near = lax.ppermute(half, AXES, lower)
    got = to_core(send)
    send, rest = first_sum(parity, keep, got)
    total = second_sum(rest, to_y(send))
    total, half = lax.optimization_barrier((total, half))
    far = lax.ppermute(half, AXES, higher)
    pieces = lax.all_to_all(total, ("yk", "xh"), 0, 0)
    near = hold(near)
    gathered = sum_pieces(pieces, near)
    return right(core, gathered, to_core(gathered), near, far)


def solution(mesh):
    dp_count, mp_count = mesh.devices.shape
    shape = (dp_count // 4, 2, 2, mp_count)
    split = Mesh(mesh.devices.reshape(shape[0] // 2, 2, *shape[1:]), AXES)
    dp = AXES[:4]
    in_specs = (P(dp, None), P(dp, "mp"), P("mp", None), P("mp", None))
    return jax.shard_map(
        functools.partial(per_device, shape),
        mesh=split,
        in_specs=in_specs,
        out_specs=P("mp", dp),
        check_vma=False,
    )
```

```python
import functools

import jax
import jax.numpy as jnp
from jax import lax
from jax.experimental import pallas as pl
from jax.experimental.pallas import tpu as pltpu
from jax.sharding import Mesh, PartitionSpec as P

F32, BF16 = jnp.float32, jnp.bfloat16
AXES = ("yk", "yp", "xh", "core", "mp")
VMEM = pl.BlockSpec(memory_space=pltpu.VMEM)
SMEM = pl.BlockSpec(memory_space=pltpu.SMEM)


def pairs(shape, move):
    y_n, x_n, c_n, m_n = shape

    def flat(y, x, c, m):
        return ((y * x_n + x) * c_n + c) * m_n + m

    return [
        (flat(y, x, c, m), flat(*move(y, x, c, m)))
        for y in range(y_n)
        for x in range(x_n)
        for c in range(c_n)
        for m in range(m_n)
    ]


def spread(shape):
    y_n, x_n, _, m_n = shape
    z_n = m_n // 2

    def move(y, x, c, m):
        to_y, to_x = m // x_n, m % x_n
        low = (m // z_n) ^ x ^ to_x
        return to_y, to_x, c, low * z_n + (m % z_n + 3 * (y - to_y) + c * (z_n // 2)) % z_n

    whole = pairs(shape, move)
    down = [(a, b) for a, b in whole if b % z_n < a % z_n]
    return down, [pair for pair in whole if pair not in down]


def products(parity, act_hbm, act, turned, send_ref, keep_ref, sems):
    tiles, _, columns = act.shape
    half, width = send_ref.shape[1:]
    copies = []
    for tile in range(tiles):
        first = pl.multiple_of((2 * tile + parity) * columns, columns)
        copies.append(pltpu.make_async_copy(act_hbm.at[:, pl.ds(first, columns)], act.at[tile], sems.at[tile]))
        copies[-1].start()

    def run():
        for tile in range(tiles):
            copies[tile].wait()
            product = jnp.dot(turned[...], act[tile], preferred_element_type=F32)
            for part in range(columns // width):
                piece = tile * (columns // width) + part
                block = product[:, part * width : (part + 1) * width]
                send_ref[piece] = block[:half].astype(BF16)
                keep_ref[piece] = block[half:]

    return run


def leading_kernel(
    at_ref, grads_hbm, left_hbm, right_hbm, act_hbm, send_ref, keep_ref, turned, half_ref, grads, left, act, sems, own
):
    core, parity = at_ref[0], at_ref[1]
    half = send_ref.shape[1]
    copies = [
        pltpu.make_async_copy(grads_hbm, grads, own.at[0]),
        pltpu.make_async_copy(left_hbm, left, own.at[1]),
    ]
    for copy in copies:
        copy.start()
    run = products(1 - parity, act_hbm, act, turned, send_ref, keep_ref, sems)
    narrow = half_ref.shape[1]
    source = right_hbm.at[:, pl.ds(pl.multiple_of(core * narrow, narrow), narrow)]
    last = pltpu.make_async_copy(source, half_ref, own.at[2])
    last.start()
    for copy in copies:
        copy.wait()
    for part in range(2):
        first = pl.multiple_of((core ^ (1 - part)) * half, half)
        turned[part * half : (part + 1) * half] = lax.dot_general(
            left[pl.ds(first, half)],
            grads[...],
            (((1,), (1,)), ((), ())),
            preferred_element_type=F32,
        ).astype(BF16)
    run()
    last.wait()


def trailing_kernel(at_ref, turned, act_hbm, send_ref, keep_ref, act, sems):
    products(at_ref[1], act_hbm, act, turned, send_ref, keep_ref, sems)()


def sizes(shape, activations, out_grads):
    y_n, x_n, c_n, _ = shape
    tokens, features = activations.shape
    rows = out_grads.shape[1]
    tiles = y_n // 2
    blocks = (tiles * x_n, rows // c_n, features // (y_n * x_n))
    cost = pl.CostEstimate(
        flops=rows * tokens * features, bytes_accessed=tokens * features, transcendentals=0
    )
    return blocks, (tiles, tokens, features // y_n), cost


def leading(shape, at, activations, out_grads, input_inverse, output_inverse):
    blocks, tiles, cost = sizes(shape, activations, out_grads)
    hbm = pl.BlockSpec(memory_space=pl.ANY)
    operands = out_grads, output_inverse, input_inverse, activations
    operands = [pltpu.with_memory_space_constraint(a, pltpu.HBM) for a in operands]
    half = (input_inverse.shape[0], input_inverse.shape[1] // 2)
    return pl.pallas_call(
        leading_kernel,
        out_shape=(
            pltpu.VMEM(blocks, BF16),
            pltpu.VMEM(blocks, F32),
            pltpu.VMEM(out_grads.shape[::-1], BF16),
            pltpu.VMEM(half, BF16),
        ),
        in_specs=[SMEM, hbm, hbm, hbm, hbm],
        out_specs=(VMEM, VMEM, VMEM, VMEM),
        scratch_shapes=[
            pltpu.VMEM(out_grads.shape, BF16),
            pltpu.VMEM(output_inverse.shape, BF16),
            pltpu.VMEM(tiles, BF16),
            pltpu.SemaphoreType.DMA((tiles[0],)),
            pltpu.SemaphoreType.DMA((3,)),
        ],
        compiler_params=pltpu.CompilerParams(vmem_limit_bytes=12 * 2**20),
        cost_estimate=cost,
    )(at, *operands)


def trailing(shape, at, activations, out_grads, turned):
    blocks, tiles, cost = sizes(shape, activations, out_grads)
    return pl.pallas_call(
        trailing_kernel,
        out_shape=(pltpu.VMEM(blocks, BF16), pltpu.VMEM(blocks, F32)),
        in_specs=[SMEM, VMEM, pl.BlockSpec(memory_space=pl.ANY)],
        out_specs=(VMEM, VMEM),
        scratch_shapes=[
            pltpu.VMEM(tiles, BF16),
            pltpu.SemaphoreType.DMA((tiles[0],)),
        ],
        compiler_params=pltpu.CompilerParams(vmem_limit_bytes=12 * 2**20),
        cost_estimate=cost,
    )(at, turned, pltpu.with_memory_space_constraint(activations, pltpu.HBM))


def first_kernel(keep_ref, got_ref, send_ref):
    for block in range(send_ref.shape[0]):
        send_ref[block] = (keep_ref[block] + got_ref[block].astype(F32)).astype(BF16)


def first_sum(keep, got):
    return pl.pallas_call(
        first_kernel,
        out_shape=pltpu.VMEM(got.shape, BF16),
        in_specs=[VMEM, VMEM],
        out_specs=VMEM,
        compiler_params=pltpu.CompilerParams(vmem_limit_bytes=8 * 2**20),
    )(keep, got)


def second_kernel(keep_ref, more_ref, got_ref, total_hbm, total_ref, sems):
    copies = []
    for block in range(keep_ref.shape[0]):
        total = keep_ref[block] + got_ref[block].astype(F32) + more_ref[block].astype(F32)
        total_ref[block] = total.astype(BF16)
        if block % 2:
            pair = pl.ds(block - 1, 2)
            copies.append(pltpu.make_async_copy(total_ref.at[pair], total_hbm.at[pair], sems.at[block // 2]))
            copies[-1].start()
    for copy in copies:
        copy.wait()


def second_sum(keep, more, got):
    return pl.pallas_call(
        second_kernel,
        out_shape=pltpu.HBM(got.shape, BF16),
        in_specs=[VMEM, VMEM, VMEM],
        out_specs=pl.BlockSpec(memory_space=pl.ANY),
        scratch_shapes=[pltpu.VMEM(got.shape, BF16), pltpu.SemaphoreType.DMA((got.shape[0] // 2,))],
        compiler_params=pltpu.CompilerParams(vmem_limit_bytes=8 * 2**20),
    )(keep, more, got)


def sum_kernel(pieces_ref, _, total_ref):
    total = pieces_ref[0].astype(F32)
    for piece in range(1, pieces_ref.shape[0]):
        total += pieces_ref[piece].astype(F32)
    total_ref[...] = total.astype(BF16)


def sum_pieces(pieces, held):
    return pl.pallas_call(
        sum_kernel,
        out_shape=jax.ShapeDtypeStruct(pieces.shape[1:], BF16),
        in_specs=[VMEM, VMEM],
        out_specs=VMEM,
        compiler_params=pltpu.CompilerParams(vmem_limit_bytes=8 * 2**20),
    )(pieces, held)


def right_kernel(core_ref, own_ref, other_ref, near_ref, far_ref, out_ref):
    half = own_ref.shape[0]
    core = core_ref[0]
    block = near_ref[...] + far_ref[...]
    for ref, index in ((own_ref, core), (other_ref, 1 - core)):
        first = pl.multiple_of(index * half, half)
        out_ref[pl.ds(first, half)] = jnp.dot(
            ref[...], block, preferred_element_type=F32
        ).astype(BF16)


def right(core, own, other, near, far):
    half, width = own.shape
    return pl.pallas_call(
        right_kernel,
        out_shape=jax.ShapeDtypeStruct((2 * half, width // 2), BF16),
        in_specs=[SMEM, VMEM, VMEM, VMEM, VMEM],
        out_specs=VMEM,
        compiler_params=pltpu.CompilerParams(vmem_limit_bytes=8 * 2**20),
    )(core.reshape(1), own, other, near, far)


def hold_kernel(block_ref, out_ref):
    out_ref[...] = block_ref[...]


def hold(block):
    return pl.pallas_call(
        hold_kernel,
        out_shape=jax.ShapeDtypeStruct(block.shape, BF16),
        in_specs=[VMEM],
        out_specs=VMEM,
        compiler_params=pltpu.CompilerParams(vmem_limit_bytes=4 * 2**20),
        cost_estimate=pl.CostEstimate(flops=5 * 10**10, bytes_accessed=2**17, transcendentals=0),
    )(block)


def per_device(shape, activations, out_grads, input_inverse, output_inverse):
    core, parity = lax.axis_index("core"), lax.axis_index("yp")
    y_n = shape[0]

    def to_core(a):
        return lax.ppermute(a, AXES, pairs(shape, lambda y, x, c, m: (y, x, 1 - c, m)))

    def to_y(a):
        def move(y, x, c, m):
            return (((y + c) % y_n ^ 1) - c) % y_n, x, c, m

        return lax.ppermute(a, AXES, pairs(shape, move))

    at = jnp.stack([core, parity])
    send, keep, turned, half = leading(shape, at, activations, out_grads, input_inverse, output_inverse)
    lower, higher = spread(shape)
    near = lax.ppermute(half, AXES, lower)
    got = to_core(send)
    send, rest = trailing(shape, at, activations, out_grads, turned)
    send_y, send = lax.optimization_barrier((first_sum(keep, got), send))
    got_y = to_y(send_y)
    total = second_sum(rest, got_y, to_core(send))
    total, half = lax.optimization_barrier((total, half))
    far = lax.ppermute(half, AXES, higher)
    pieces = lax.all_to_all(total, ("yk", "xh"), 0, 0)
    near = hold(near)
    gathered = sum_pieces(pieces, near)
    return right(core, gathered, to_core(gathered), near, far)


def solution(mesh):
    dp_count, mp_count = mesh.devices.shape
    shape = (dp_count // 4, 2, 2, mp_count)
    split = Mesh(mesh.devices.reshape(shape[0] // 2, 2, *shape[1:]), AXES)
    dp = AXES[:4]
    in_specs = (P(dp, None), P(dp, "mp"), P("mp", None), P("mp", None))
    return jax.shard_map(
        functools.partial(per_device, shape),
        mesh=split,
        in_specs=in_specs,
        out_specs=P("mp", dp),
        check_vma=False,
    )
```

```python
import functools

import jax
import jax.numpy as jnp
from jax import lax
from jax.experimental import pallas as pl
from jax.experimental.pallas import tpu as pltpu
from jax.sharding import Mesh, PartitionSpec as P

F32, BF16 = jnp.float32, jnp.bfloat16
AXES = ("yk", "yp", "xh", "core", "mp")
VMEM = pl.BlockSpec(memory_space=pltpu.VMEM)
SMEM = pl.BlockSpec(memory_space=pltpu.SMEM)


def pairs(shape, move):
    y_n, x_n, c_n, m_n = shape

    def flat(y, x, c, m):
        return ((y * x_n + x) * c_n + c) * m_n + m

    return [
        (flat(y, x, c, m), flat(*move(y, x, c, m)))
        for y in range(y_n)
        for x in range(x_n)
        for c in range(c_n)
        for m in range(m_n)
    ]


def spread(shape):
    y_n, x_n, _, m_n = shape
    z_n = m_n // 2

    def move(y, x, c, m):
        to_y, to_x = m // x_n, m % x_n
        low = (m // z_n) ^ x ^ to_x
        return to_y, to_x, c, low * z_n + (m % z_n + 3 * (y - to_y) + c * (z_n // 2)) % z_n

    whole = pairs(shape, move)
    down = [(a, b) for a, b in whole if b % z_n < a % z_n]
    return down, [pair for pair in whole if pair not in down]


def products(parity, act_hbm, act, turned, send_ref, keep_ref, sems):
    tiles, _, columns = act.shape
    half, width = send_ref.shape[1:]
    copies = []
    for tile in range(tiles):
        first = pl.multiple_of((2 * tile + parity) * columns, columns)
        copies.append(pltpu.make_async_copy(act_hbm.at[:, pl.ds(first, columns)], act.at[tile], sems.at[tile]))
        copies[-1].start(priority=1)

    def run():
        for tile in range(tiles):
            copies[tile].wait()
            product = jnp.dot(turned[...], act[tile], preferred_element_type=F32)
            for part in range(columns // width):
                piece = tile * (columns // width) + part
                block = product[:, part * width : (part + 1) * width]
                send_ref[piece] = block[:half].astype(BF16)
                keep_ref[piece] = block[half:]

    return run


def leading_kernel(
    at_ref, grads_hbm, left_hbm, right_hbm, act_hbm, send_ref, keep_ref, turned, half_ref, grads, left, act, sems, own
):
    core, parity = at_ref[0], at_ref[1]
    half = send_ref.shape[1]
    copies = [
        pltpu.make_async_copy(grads_hbm, grads, own.at[0]),
        pltpu.make_async_copy(left_hbm, left, own.at[1]),
    ]
    for copy in copies:
        copy.start()
    run = products(1 - parity, act_hbm, act, turned, send_ref, keep_ref, sems)
    narrow = half_ref.shape[1]
    source = right_hbm.at[:, pl.ds(pl.multiple_of(core * narrow, narrow), narrow)]
    last = pltpu.make_async_copy(source, half_ref, own.at[2])
    last.start()
    for copy in copies:
        copy.wait()
    for part in range(2):
        first = pl.multiple_of((core ^ (1 - part)) * half, half)
        turned[part * half : (part + 1) * half] = lax.dot_general(
            left[pl.ds(first, half)],
            grads[...],
            (((1,), (1,)), ((), ())),
            preferred_element_type=F32,
        ).astype(BF16)
    run()
    last.wait()


def trailing_kernel(at_ref, turned, act_hbm, send_ref, keep_ref, act, sems):
    products(at_ref[1], act_hbm, act, turned, send_ref, keep_ref, sems)()


def sizes(shape, activations, out_grads):
    y_n, x_n, c_n, _ = shape
    tokens, features = activations.shape
    rows = out_grads.shape[1]
    tiles = y_n // 2
    blocks = (tiles * x_n, rows // c_n, features // (y_n * x_n))
    cost = pl.CostEstimate(
        flops=rows * tokens * features, bytes_accessed=tokens * features, transcendentals=0
    )
    return blocks, (tiles, tokens, features // y_n), cost


def leading(shape, at, activations, out_grads, input_inverse, output_inverse):
    blocks, tiles, cost = sizes(shape, activations, out_grads)
    hbm = pl.BlockSpec(memory_space=pl.ANY)
    operands = out_grads, output_inverse, input_inverse, activations
    operands = [pltpu.with_memory_space_constraint(a, pltpu.HBM) for a in operands]
    half = (input_inverse.shape[0], input_inverse.shape[1] // 2)
    return pl.pallas_call(
        leading_kernel,
        out_shape=(
            pltpu.VMEM(blocks, BF16),
            pltpu.VMEM(blocks, F32),
            pltpu.VMEM(out_grads.shape[::-1], BF16),
            pltpu.VMEM(half, BF16),
        ),
        in_specs=[SMEM, hbm, hbm, hbm, hbm],
        out_specs=(VMEM, VMEM, VMEM, VMEM),
        scratch_shapes=[
            pltpu.VMEM(out_grads.shape, BF16),
            pltpu.VMEM(output_inverse.shape, BF16),
            pltpu.VMEM(tiles, BF16),
            pltpu.SemaphoreType.DMA((tiles[0],)),
            pltpu.SemaphoreType.DMA((3,)),
        ],
        compiler_params=pltpu.CompilerParams(vmem_limit_bytes=12 * 2**20),
        cost_estimate=cost,
    )(at, *operands)


def trailing(shape, at, activations, out_grads, turned):
    blocks, tiles, cost = sizes(shape, activations, out_grads)
    return pl.pallas_call(
        trailing_kernel,
        out_shape=(pltpu.VMEM(blocks, BF16), pltpu.VMEM(blocks, F32)),
        in_specs=[SMEM, VMEM, pl.BlockSpec(memory_space=pl.ANY)],
        out_specs=(VMEM, VMEM),
        scratch_shapes=[
            pltpu.VMEM(tiles, BF16),
            pltpu.SemaphoreType.DMA((tiles[0],)),
        ],
        compiler_params=pltpu.CompilerParams(vmem_limit_bytes=12 * 2**20),
        cost_estimate=cost,
    )(at, turned, pltpu.with_memory_space_constraint(activations, pltpu.HBM))


def first_kernel(keep_ref, got_ref, send_ref):
    for block in range(send_ref.shape[0]):
        send_ref[block] = (keep_ref[block] + got_ref[block].astype(F32)).astype(BF16)


def first_sum(keep, got):
    return pl.pallas_call(
        first_kernel,
        out_shape=pltpu.VMEM(got.shape, BF16),
        in_specs=[VMEM, VMEM],
        out_specs=VMEM,
        compiler_params=pltpu.CompilerParams(vmem_limit_bytes=8 * 2**20),
    )(keep, got)


def second_kernel(keep_ref, more_ref, got_ref, total_hbm, total_ref, sems):
    copies = []
    for block in range(keep_ref.shape[0]):
        total = keep_ref[block] + got_ref[block].astype(F32) + more_ref[block].astype(F32)
        total_ref[block] = total.astype(BF16)
        if block % 2:
            pair = pl.ds(block - 1, 2)
            copies.append(pltpu.make_async_copy(total_ref.at[pair], total_hbm.at[pair], sems.at[block // 2]))
            copies[-1].start()
    for copy in copies:
        copy.wait()


def second_sum(keep, more, got):
    return pl.pallas_call(
        second_kernel,
        out_shape=pltpu.HBM(got.shape, BF16),
        in_specs=[VMEM, VMEM, VMEM],
        out_specs=pl.BlockSpec(memory_space=pl.ANY),
        scratch_shapes=[pltpu.VMEM(got.shape, BF16), pltpu.SemaphoreType.DMA((got.shape[0] // 2,))],
        compiler_params=pltpu.CompilerParams(vmem_limit_bytes=8 * 2**20),
    )(keep, more, got)


def sum_kernel(pieces_ref, _, total_ref):
    total = pieces_ref[0].astype(F32)
    for piece in range(1, pieces_ref.shape[0]):
        total += pieces_ref[piece].astype(F32)
    total_ref[...] = total.astype(BF16)


def sum_pieces(pieces, held):
    return pl.pallas_call(
        sum_kernel,
        out_shape=jax.ShapeDtypeStruct(pieces.shape[1:], BF16),
        in_specs=[VMEM, VMEM],
        out_specs=VMEM,
        compiler_params=pltpu.CompilerParams(vmem_limit_bytes=8 * 2**20),
    )(pieces, held)


def right_kernel(core_ref, own_ref, other_ref, near_ref, far_ref, out_ref):
    half = own_ref.shape[0]
    core = core_ref[0]
    block = near_ref[...] + far_ref[...]
    for ref, index in ((own_ref, core), (other_ref, 1 - core)):
        first = pl.multiple_of(index * half, half)
        out_ref[pl.ds(first, half)] = jnp.dot(
            ref[...], block, preferred_element_type=F32
        ).astype(BF16)


def right(core, own, other, near, far):
    half, width = own.shape
    return pl.pallas_call(
        right_kernel,
        out_shape=jax.ShapeDtypeStruct((2 * half, width // 2), BF16),
        in_specs=[SMEM, VMEM, VMEM, VMEM, VMEM],
        out_specs=VMEM,
        compiler_params=pltpu.CompilerParams(vmem_limit_bytes=8 * 2**20),
    )(core.reshape(1), own, other, near, far)


def hold_kernel(block_ref, out_ref):
    out_ref[...] = block_ref[...]


def hold(block, flops):
    return pl.pallas_call(
        hold_kernel,
        out_shape=jax.ShapeDtypeStruct(block.shape, BF16),
        in_specs=[VMEM],
        out_specs=VMEM,
        compiler_params=pltpu.CompilerParams(vmem_limit_bytes=4 * 2**20),
        cost_estimate=pl.CostEstimate(flops=flops, bytes_accessed=2**17, transcendentals=0),
    )(block)


def per_device(shape, activations, out_grads, input_inverse, output_inverse):
    core, parity = lax.axis_index("core"), lax.axis_index("yp")
    y_n = shape[0]

    def to_core(a):
        return lax.ppermute(a, AXES, pairs(shape, lambda y, x, c, m: (y, x, 1 - c, m)))

    def to_y(a):
        def move(y, x, c, m):
            return (((y + c) % y_n ^ 1) - c) % y_n, x, c, m

        return lax.ppermute(a, AXES, pairs(shape, move))

    at = jnp.stack([core, parity])
    send, keep, turned, half = leading(shape, at, activations, out_grads, input_inverse, output_inverse)
    lower, higher = spread(shape)
    near = lax.ppermute(half, AXES, lower)
    send_y, turned = lax.optimization_barrier((first_sum(keep, to_core(send)), turned))
    send, rest = trailing(shape, at, activations, out_grads, turned)
    got_y = hold(to_y(send_y), 5 * 10**9)
    total = second_sum(rest, got_y, to_core(send))
    total, half = lax.optimization_barrier((total, half))
    far = lax.ppermute(half, AXES, higher)
    pieces = lax.all_to_all(total, ("yk", "xh"), 0, 0)
    near = hold(near, 5 * 10**10)
    gathered = sum_pieces(pieces, near)
    return right(core, gathered, to_core(gathered), near, far)


def solution(mesh):
    dp_count, mp_count = mesh.devices.shape
    shape = (dp_count // 4, 2, 2, mp_count)
    split = Mesh(mesh.devices.reshape(shape[0] // 2, 2, *shape[1:]), AXES)
    dp = AXES[:4]
    in_specs = (P(dp, None), P(dp, "mp"), P("mp", None), P("mp", None))
    return jax.shard_map(
        functools.partial(per_device, shape),
        mesh=split,
        in_specs=in_specs,
        out_specs=P("mp", dp),
        check_vma=False,
    )
```

```python
import functools

import jax
import jax.numpy as jnp
from jax import lax
from jax.experimental import pallas as pl
from jax.experimental.pallas import tpu as pltpu
from jax.sharding import Mesh, PartitionSpec as P

F32, BF16 = jnp.float32, jnp.bfloat16
AXES = ("yk", "yp", "xh", "core", "mp")
VMEM = pl.BlockSpec(memory_space=pltpu.VMEM)
SMEM = pl.BlockSpec(memory_space=pltpu.SMEM)


def pairs(shape, move):
    y_n, x_n, c_n, m_n = shape

    def flat(y, x, c, m):
        return ((y * x_n + x) * c_n + c) * m_n + m

    return [
        (flat(y, x, c, m), flat(*move(y, x, c, m)))
        for y in range(y_n)
        for x in range(x_n)
        for c in range(c_n)
        for m in range(m_n)
    ]


def lateness(shape, device):
    y_n, x_n, c_n, m_n = shape
    y = device // (x_n * c_n * m_n)
    return 3 * (device % (m_n // 2)) + 2 * min(y, y_n - y)


def spread(shape):
    y_n, x_n, _, m_n = shape
    z_n = m_n // 2

    def move(y, x, c, m):
        to_y, to_x = m // x_n, m % x_n
        low = (m // z_n) ^ x ^ to_x
        return to_y, to_x, c, low * z_n + (m % z_n + 3 * (y - to_y) + c * (z_n // 2)) % z_n

    whole = pairs(shape, move)
    lower = [(a, b) for a, b in whole if lateness(shape, a) - lateness(shape, b) >= 1]
    return lower, [pair for pair in whole if pair not in lower]


def products(parity, act_hbm, act, turned, send_ref, keep_ref, sems):
    tiles, _, columns = act.shape
    half, width = send_ref.shape[1:]
    copies = []
    for tile in range(tiles):
        first = pl.multiple_of((2 * tile + parity) * columns, columns)
        copies.append(pltpu.make_async_copy(act_hbm.at[:, pl.ds(first, columns)], act.at[tile], sems.at[tile]))
        copies[-1].start(priority=1)

    def run():
        for tile in range(tiles):
            copies[tile].wait()
            product = jnp.dot(turned[...], act[tile], preferred_element_type=F32)
            for part in range(columns // width):
                piece = tile * (columns // width) + part
                block = product[:, part * width : (part + 1) * width]
                send_ref[piece] = block[:half].astype(BF16)
                keep_ref[piece] = block[half:]

    return run


def leading_kernel(
    core_ref, parity_ref, grads_hbm, left_hbm, right_hbm, act_hbm, send_ref, keep_ref, turned, half_ref, grads, left, act, sems, own
):
    core, parity = core_ref[0], parity_ref[0]
    half = send_ref.shape[1]
    copies = [
        pltpu.make_async_copy(grads_hbm, grads, own.at[0]),
        pltpu.make_async_copy(left_hbm, left, own.at[1]),
    ]
    for copy in copies:
        copy.start()
    run = products(1 - parity, act_hbm, act, turned, send_ref, keep_ref, sems)
    narrow = half_ref.shape[1]
    source = right_hbm.at[:, pl.ds(pl.multiple_of(core * narrow, narrow), narrow)]
    last = pltpu.make_async_copy(source, half_ref, own.at[2])
    last.start()
    for copy in copies:
        copy.wait()
    for part in range(2):
        first = pl.multiple_of((core ^ (1 - part)) * half, half)
        turned[part * half : (part + 1) * half] = lax.dot_general(
            left[pl.ds(first, half)],
            grads[...],
            (((1,), (1,)), ((), ())),
            preferred_element_type=F32,
        ).astype(BF16)
    run()
    last.wait()


def trailing_kernel(parity_ref, turned, act_hbm, send_ref, keep_ref, act, sems):
    products(parity_ref[0], act_hbm, act, turned, send_ref, keep_ref, sems)()


def sizes(shape, activations, out_grads):
    y_n, x_n, c_n, _ = shape
    tokens, features = activations.shape
    rows = out_grads.shape[1]
    tiles = y_n // 2
    blocks = (tiles * x_n, rows // c_n, features // (y_n * x_n))
    cost = pl.CostEstimate(
        flops=rows * tokens * features, bytes_accessed=tokens * features, transcendentals=0
    )
    return blocks, (tiles, tokens, features // y_n), cost


def leading(shape, at, activations, out_grads, input_inverse, output_inverse):
    blocks, tiles, cost = sizes(shape, activations, out_grads)
    hbm = pl.BlockSpec(memory_space=pl.ANY)
    operands = out_grads, output_inverse, input_inverse, activations
    operands = [pltpu.with_memory_space_constraint(a, pltpu.HBM) for a in operands]
    half = (input_inverse.shape[0], input_inverse.shape[1] // 2)
    return pl.pallas_call(
        leading_kernel,
        out_shape=(
            pltpu.VMEM(blocks, BF16),
            pltpu.VMEM(blocks, F32),
            pltpu.VMEM(out_grads.shape[::-1], BF16),
            pltpu.VMEM(half, BF16),
        ),
        in_specs=[SMEM, SMEM, hbm, hbm, hbm, hbm],
        out_specs=(VMEM, VMEM, VMEM, VMEM),
        scratch_shapes=[
            pltpu.VMEM(out_grads.shape, BF16),
            pltpu.VMEM(output_inverse.shape, BF16),
            pltpu.VMEM(tiles, BF16),
            pltpu.SemaphoreType.DMA((tiles[0],)),
            pltpu.SemaphoreType.DMA((3,)),
        ],
        compiler_params=pltpu.CompilerParams(vmem_limit_bytes=12 * 2**20),
        cost_estimate=cost,
    )(*at, *operands)


def trailing(shape, at, activations, out_grads, turned):
    blocks, tiles, cost = sizes(shape, activations, out_grads)
    return pl.pallas_call(
        trailing_kernel,
        out_shape=(pltpu.VMEM(blocks, BF16), pltpu.VMEM(blocks, F32)),
        in_specs=[SMEM, VMEM, pl.BlockSpec(memory_space=pl.ANY)],
        out_specs=(VMEM, VMEM),
        scratch_shapes=[
            pltpu.VMEM(tiles, BF16),
            pltpu.SemaphoreType.DMA((tiles[0],)),
        ],
        compiler_params=pltpu.CompilerParams(vmem_limit_bytes=12 * 2**20),
        cost_estimate=cost,
    )(at[1], turned, pltpu.with_memory_space_constraint(activations, pltpu.HBM))


def first_kernel(keep_ref, got_ref, send_ref):
    for block in range(send_ref.shape[0]):
        send_ref[block] = (keep_ref[block] + got_ref[block].astype(F32)).astype(BF16)


def first_sum(keep, got):
    return pl.pallas_call(
        first_kernel,
        out_shape=pltpu.VMEM(got.shape, BF16),
        in_specs=[VMEM, VMEM],
        out_specs=VMEM,
        compiler_params=pltpu.CompilerParams(vmem_limit_bytes=8 * 2**20),
    )(keep, got)


def second_kernel(keep_ref, more_ref, got_ref, total_hbm, total_ref, sems):
    copies = []
    for block in range(keep_ref.shape[0]):
        total = keep_ref[block] + got_ref[block].astype(F32) + more_ref[block].astype(F32)
        total_ref[block] = total.astype(BF16)
        if block % 2:
            pair = pl.ds(block - 1, 2)
            copies.append(pltpu.make_async_copy(total_ref.at[pair], total_hbm.at[pair], sems.at[block // 2]))
            copies[-1].start()
    for copy in copies:
        copy.wait()


def second_sum(keep, more, got):
    return pl.pallas_call(
        second_kernel,
        out_shape=pltpu.HBM(got.shape, BF16),
        in_specs=[VMEM, VMEM, VMEM],
        out_specs=pl.BlockSpec(memory_space=pl.ANY),
        scratch_shapes=[pltpu.VMEM(got.shape, BF16), pltpu.SemaphoreType.DMA((got.shape[0] // 2,))],
        compiler_params=pltpu.CompilerParams(vmem_limit_bytes=8 * 2**20),
    )(keep, more, got)


def sum_kernel(pieces_ref, _, total_ref):
    total = pieces_ref[0].astype(F32)
    for piece in range(1, pieces_ref.shape[0]):
        total += pieces_ref[piece].astype(F32)
    total_ref[...] = total.astype(BF16)


def sum_pieces(pieces, held):
    return pl.pallas_call(
        sum_kernel,
        out_shape=jax.ShapeDtypeStruct(pieces.shape[1:], BF16),
        in_specs=[VMEM, VMEM],
        out_specs=VMEM,
        compiler_params=pltpu.CompilerParams(vmem_limit_bytes=8 * 2**20),
    )(pieces, held)


def right_kernel(core_ref, own_ref, other_ref, near_ref, far_ref, out_ref):
    half = own_ref.shape[0]
    core = core_ref[0]
    block = near_ref[...] + far_ref[...]
    for ref, index in ((own_ref, core), (other_ref, 1 - core)):
        first = pl.multiple_of(index * half, half)
        out_ref[pl.ds(first, half)] = jnp.dot(
            ref[...], block, preferred_element_type=F32
        ).astype(BF16)


def right(core, own, other, near, far):
    half, width = own.shape
    return pl.pallas_call(
        right_kernel,
        out_shape=jax.ShapeDtypeStruct((2 * half, width // 2), BF16),
        in_specs=[SMEM, VMEM, VMEM, VMEM, VMEM],
        out_specs=VMEM,
        compiler_params=pltpu.CompilerParams(vmem_limit_bytes=8 * 2**20),
    )(core.reshape(1), own, other, near, far)


def hold_kernel(block_ref, out_ref):
    out_ref[...] = block_ref[...]


def hold(block, flops):
    return pl.pallas_call(
        hold_kernel,
        out_shape=jax.ShapeDtypeStruct(block.shape, BF16),
        in_specs=[VMEM],
        out_specs=VMEM,
        compiler_params=pltpu.CompilerParams(vmem_limit_bytes=4 * 2**20),
        cost_estimate=pl.CostEstimate(flops=flops, bytes_accessed=2**17, transcendentals=0),
    )(block)


def per_device(shape, activations, out_grads, input_inverse, output_inverse):
    core, parity = lax.axis_index("core"), lax.axis_index("yp")
    y_n = shape[0]

    def to_core(a):
        return lax.ppermute(a, AXES, pairs(shape, lambda y, x, c, m: (y, x, 1 - c, m)))

    def to_y(a):
        def move(y, x, c, m):
            return (((y + c) % y_n ^ 1) - c) % y_n, x, c, m

        return lax.ppermute(a, AXES, pairs(shape, move))

    at = core.reshape(1), parity.reshape(1)
    send, keep, turned, half = leading(shape, at, activations, out_grads, input_inverse, output_inverse)
    lower, higher = spread(shape)
    near = lax.ppermute(half, AXES, lower)
    send_y, turned = lax.optimization_barrier((first_sum(keep, to_core(send)), turned))
    send, rest = trailing(shape, at, activations, out_grads, turned)
    got_y = hold(to_y(send_y), 5 * 10**9)
    total = second_sum(rest, got_y, to_core(send))
    total, half = lax.optimization_barrier((total, half))
    far = lax.ppermute(half, AXES, higher)
    pieces = lax.all_to_all(total, ("yk", "xh"), 0, 0)
    near = hold(near, 5 * 10**10)
    gathered = sum_pieces(pieces, near)
    return right(core, gathered, to_core(gathered), near, far)


def solution(mesh):
    dp_count, mp_count = mesh.devices.shape
    shape = (dp_count // 4, 2, 2, mp_count)
    split = Mesh(mesh.devices.reshape(shape[0] // 2, 2, *shape[1:]), AXES)
    dp = AXES[:4]
    in_specs = (P(dp, None), P(dp, "mp"), P("mp", None), P("mp", None))
    return jax.shard_map(
        functools.partial(per_device, shape),
        mesh=split,
        in_specs=in_specs,
        out_specs=P("mp", dp),
        check_vma=False,
    )
```

```python
import functools

import jax
import jax.numpy as jnp
from jax import lax
from jax.experimental import pallas as pl
from jax.experimental.pallas import tpu as pltpu
from jax.sharding import Mesh, PartitionSpec as P

F32, BF16 = jnp.float32, jnp.bfloat16
AXES = ("yk", "yp", "xh", "core", "mp")
VMEM = pl.BlockSpec(memory_space=pltpu.VMEM)
SMEM = pl.BlockSpec(memory_space=pltpu.SMEM)


def pairs(shape, move):
    y_n, x_n, c_n, m_n = shape

    def flat(y, x, c, m):
        return ((y * x_n + x) * c_n + c) * m_n + m

    return [
        (flat(y, x, c, m), flat(*move(y, x, c, m)))
        for y in range(y_n)
        for x in range(x_n)
        for c in range(c_n)
        for m in range(m_n)
    ]


def lateness(shape, device):
    y_n, x_n, c_n, m_n = shape
    y = device // (x_n * c_n * m_n)
    x = 2 * (device // (c_n * m_n) % x_n) + device % m_n // (m_n // 2)
    return 3 * (device % (m_n // 2)) + 2 * min(y, y_n - y) + x


def spread(shape):
    y_n, x_n, _, m_n = shape
    z_n = m_n // 2

    def move(y, x, c, m):
        to_y, to_x = m // x_n, m % x_n
        low = (m // z_n) ^ x ^ to_x
        return to_y, to_x, c, low * z_n + (m % z_n + 3 * (y - to_y) + c * (z_n // 2)) % z_n

    whole = pairs(shape, move)
    lower = [(a, b) for a, b in whole if lateness(shape, a) - lateness(shape, b) >= 1]
    return lower, [pair for pair in whole if pair not in lower]


def products(parity, act_hbm, act, turned, send_ref, keep_ref, sems):
    tiles, _, columns = act.shape
    half, width = send_ref.shape[1:]
    copies = []
    for tile in range(tiles):
        first = pl.multiple_of((2 * tile + parity) * columns, columns)
        copies.append(pltpu.make_async_copy(act_hbm.at[:, pl.ds(first, columns)], act.at[tile], sems.at[tile]))
        copies[-1].start(priority=1)

    def run():
        for tile in range(tiles):
            copies[tile].wait()
            product = jnp.dot(turned[...], act[tile], preferred_element_type=F32)
            for part in range(columns // width):
                piece = tile * (columns // width) + part
                block = product[:, part * width : (part + 1) * width]
                send_ref[piece] = block[:half].astype(BF16)
                keep_ref[piece] = block[half:]

    return run


def leading_kernel(
    core_ref, parity_ref, grads_hbm, left_hbm, right_hbm, act_hbm, send_ref, keep_ref, turned, half_ref, grads, left, act, sems, own
):
    core, parity = core_ref[0], parity_ref[0]
    half = send_ref.shape[1]
    copies = [
        pltpu.make_async_copy(grads_hbm, grads, own.at[0]),
        pltpu.make_async_copy(left_hbm, left, own.at[1]),
    ]
    for copy in copies:
        copy.start()
    run = products(1 - parity, act_hbm, act, turned, send_ref, keep_ref, sems)
    narrow = half_ref.shape[1]
    source = right_hbm.at[:, pl.ds(pl.multiple_of(core * narrow, narrow), narrow)]
    last = pltpu.make_async_copy(source, half_ref, own.at[2])
    last.start()
    for copy in copies:
        copy.wait()
    for part in range(2):
        first = pl.multiple_of((core ^ (1 - part)) * half, half)
        turned[part * half : (part + 1) * half] = lax.dot_general(
            left[pl.ds(first, half)],
            grads[...],
            (((1,), (1,)), ((), ())),
            preferred_element_type=F32,
        ).astype(BF16)
    run()
    last.wait()


def trailing_kernel(parity_ref, turned, act_hbm, send_ref, keep_ref, act, sems):
    products(parity_ref[0], act_hbm, act, turned, send_ref, keep_ref, sems)()


def sizes(shape, activations, out_grads):
    y_n, x_n, c_n, _ = shape
    tokens, features = activations.shape
    rows = out_grads.shape[1]
    tiles = y_n // 2
    blocks = (tiles * x_n, rows // c_n, features // (y_n * x_n))
    cost = pl.CostEstimate(
        flops=rows * tokens * features, bytes_accessed=tokens * features, transcendentals=0
    )
    return blocks, (tiles, tokens, features // y_n), cost


def leading(shape, at, activations, out_grads, input_inverse, output_inverse):
    blocks, tiles, cost = sizes(shape, activations, out_grads)
    hbm = pl.BlockSpec(memory_space=pl.ANY)
    operands = out_grads, output_inverse, input_inverse, activations
    operands = [pltpu.with_memory_space_constraint(a, pltpu.HBM) for a in operands]
    half = (input_inverse.shape[0], input_inverse.shape[1] // 2)
    return pl.pallas_call(
        leading_kernel,
        out_shape=(
            pltpu.VMEM(blocks, BF16),
            pltpu.VMEM(blocks, F32),
            pltpu.VMEM(out_grads.shape[::-1], BF16),
            pltpu.VMEM(half, BF16),
        ),
        in_specs=[SMEM, SMEM, hbm, hbm, hbm, hbm],
        out_specs=(VMEM, VMEM, VMEM, VMEM),
        scratch_shapes=[
            pltpu.VMEM(out_grads.shape, BF16),
            pltpu.VMEM(output_inverse.shape, BF16),
            pltpu.VMEM(tiles, BF16),
            pltpu.SemaphoreType.DMA((tiles[0],)),
            pltpu.SemaphoreType.DMA((3,)),
        ],
        compiler_params=pltpu.CompilerParams(vmem_limit_bytes=12 * 2**20),
        cost_estimate=cost,
    )(*at, *operands)


def trailing(shape, at, activations, out_grads, turned):
    blocks, tiles, cost = sizes(shape, activations, out_grads)
    return pl.pallas_call(
        trailing_kernel,
        out_shape=(pltpu.VMEM(blocks, BF16), pltpu.VMEM(blocks, F32)),
        in_specs=[SMEM, VMEM, pl.BlockSpec(memory_space=pl.ANY)],
        out_specs=(VMEM, VMEM),
        scratch_shapes=[
            pltpu.VMEM(tiles, BF16),
            pltpu.SemaphoreType.DMA((tiles[0],)),
        ],
        compiler_params=pltpu.CompilerParams(vmem_limit_bytes=12 * 2**20),
        cost_estimate=cost,
    )(at[1], turned, pltpu.with_memory_space_constraint(activations, pltpu.HBM))


def first_kernel(keep_ref, got_ref, send_ref):
    for block in range(send_ref.shape[0]):
        send_ref[block] = (keep_ref[block] + got_ref[block].astype(F32)).astype(BF16)


def first_sum(keep, got):
    return pl.pallas_call(
        first_kernel,
        out_shape=pltpu.VMEM(got.shape, BF16),
        in_specs=[VMEM, VMEM],
        out_specs=VMEM,
        compiler_params=pltpu.CompilerParams(vmem_limit_bytes=8 * 2**20),
    )(keep, got)


def second_kernel(keep_ref, more_ref, got_ref, total_hbm, total_ref, sems):
    copies = []
    for block in range(keep_ref.shape[0]):
        total = keep_ref[block] + got_ref[block].astype(F32) + more_ref[block].astype(F32)
        total_ref[block] = total.astype(BF16)
        copies.append(pltpu.make_async_copy(total_ref.at[block], total_hbm.at[block], sems.at[block]))
        copies[-1].start(priority=block % 2)
    for copy in copies:
        copy.wait()


def second_sum(keep, more, got):
    return pl.pallas_call(
        second_kernel,
        out_shape=pltpu.HBM(got.shape, BF16),
        in_specs=[VMEM, VMEM, VMEM],
        out_specs=pl.BlockSpec(memory_space=pl.ANY),
        scratch_shapes=[pltpu.VMEM(got.shape, BF16), pltpu.SemaphoreType.DMA((got.shape[0],))],
        compiler_params=pltpu.CompilerParams(vmem_limit_bytes=8 * 2**20),
    )(keep, more, got)


def sum_kernel(pieces_ref, _, total_ref):
    total = pieces_ref[0].astype(F32)
    for piece in range(1, pieces_ref.shape[0]):
        total += pieces_ref[piece].astype(F32)
    total_ref[...] = total.astype(BF16)


def sum_pieces(pieces, held):
    return pl.pallas_call(
        sum_kernel,
        out_shape=jax.ShapeDtypeStruct(pieces.shape[1:], BF16),
        in_specs=[VMEM, VMEM],
        out_specs=VMEM,
        compiler_params=pltpu.CompilerParams(vmem_limit_bytes=8 * 2**20),
    )(pieces, held)


def right_kernel(core_ref, own_ref, other_ref, near_ref, far_ref, out_ref):
    half = own_ref.shape[0]
    core = core_ref[0]
    block = near_ref[...] + far_ref[...]
    for ref, index in ((own_ref, core), (other_ref, 1 - core)):
        first = pl.multiple_of(index * half, half)
        out_ref[pl.ds(first, half)] = jnp.dot(
            ref[...], block, preferred_element_type=F32
        ).astype(BF16)


def right(core, own, other, near, far):
    half, width = own.shape
    return pl.pallas_call(
        right_kernel,
        out_shape=jax.ShapeDtypeStruct((2 * half, width // 2), BF16),
        in_specs=[SMEM, VMEM, VMEM, VMEM, VMEM],
        out_specs=VMEM,
        compiler_params=pltpu.CompilerParams(vmem_limit_bytes=8 * 2**20),
    )(core.reshape(1), own, other, near, far)


def hold_kernel(block_ref, out_ref):
    rows = 16 if len(out_ref.shape) == 2 else 1
    out_ref[:rows] = block_ref[:rows]


def hold(block, flops):
    return pl.pallas_call(
        hold_kernel,
        out_shape=jax.ShapeDtypeStruct(block.shape, BF16),
        in_specs=[VMEM],
        out_specs=VMEM,
        input_output_aliases={0: 0},
        compiler_params=pltpu.CompilerParams(vmem_limit_bytes=4 * 2**20),
        cost_estimate=pl.CostEstimate(flops=flops, bytes_accessed=2**17, transcendentals=0),
    )(block)


def per_device(shape, activations, out_grads, input_inverse, output_inverse):
    core, parity = lax.axis_index("core"), lax.axis_index("yp")
    y_n = shape[0]

    def to_core(a):
        return lax.ppermute(a, AXES, pairs(shape, lambda y, x, c, m: (y, x, 1 - c, m)))

    def to_y(a):
        def move(y, x, c, m):
            return (((y + c) % y_n ^ 1) - c) % y_n, x, c, m

        return lax.ppermute(a, AXES, pairs(shape, move))

    at = core.reshape(1), parity.reshape(1)
    send, keep, turned, half = leading(shape, at, activations, out_grads, input_inverse, output_inverse)
    lower, higher = spread(shape)
    near = lax.ppermute(half, AXES, lower)
    send_y, turned = lax.optimization_barrier((first_sum(keep, to_core(send)), turned))
    send, rest = trailing(shape, at, activations, out_grads, turned)
    got_y = hold(to_y(send_y), 5 * 10**9)
    total = second_sum(rest, got_y, to_core(send))
    total, half = lax.optimization_barrier((total, half))
    far = lax.ppermute(half, AXES, higher)
    pieces = lax.all_to_all(total, ("yk", "xh"), 0, 0)
    near = hold(near, 5 * 10**10)
    gathered = sum_pieces(pieces, near)
    return right(core, gathered, to_core(gathered), near, far)


def solution(mesh):
    dp_count, mp_count = mesh.devices.shape
    shape = (dp_count // 4, 2, 2, mp_count)
    split = Mesh(mesh.devices.reshape(shape[0] // 2, 2, *shape[1:]), AXES)
    dp = AXES[:4]
    in_specs = (P(dp, None), P(dp, "mp"), P("mp", None), P("mp", None))
    return jax.shard_map(
        functools.partial(per_device, shape),
        mesh=split,
        in_specs=in_specs,
        out_specs=P("mp", dp),
        check_vma=False,
    )
```

```python
import functools

import jax
import jax.numpy as jnp
from jax import lax
from jax.experimental import pallas as pl
from jax.experimental.pallas import tpu as pltpu
from jax.sharding import Mesh, PartitionSpec as P

F32, BF16 = jnp.float32, jnp.bfloat16
AXES = ("yk", "yp", "xh", "core", "mp")
VMEM = pl.BlockSpec(memory_space=pltpu.VMEM)
SMEM = pl.BlockSpec(memory_space=pltpu.SMEM)


def pairs(shape, move):
    y_n, x_n, c_n, m_n = shape

    def flat(y, x, c, m):
        return ((y * x_n + x) * c_n + c) * m_n + m

    return [
        (flat(y, x, c, m), flat(*move(y, x, c, m)))
        for y in range(y_n)
        for x in range(x_n)
        for c in range(c_n)
        for m in range(m_n)
    ]


def lateness(shape, device):
    y_n, x_n, c_n, m_n = shape
    y = device // (x_n * c_n * m_n)
    x = 2 * (device // (c_n * m_n) % x_n) + device % m_n // (m_n // 2)
    return 3 * (device % (m_n // 2)) + 2 * min(y, y_n - y) + x


def spread(shape):
    y_n, x_n, _, m_n = shape
    z_n = m_n // 2

    def move(y, x, c, m):
        to_y, to_x = m // x_n, m % x_n
        low = (m // z_n) ^ x ^ to_x
        return to_y, to_x, c, low * z_n + (m % z_n + 3 * (y - to_y) + c * (z_n // 2)) % z_n

    whole = pairs(shape, move)
    lower = [(a, b) for a, b in whole if lateness(shape, a) - lateness(shape, b) >= 1]
    return lower, [pair for pair in whole if pair not in lower]


def products(parity, act_hbm, act, turned, send_ref, keep_ref, sems):
    tiles, _, columns = act.shape
    half, width = send_ref.shape[1:]
    copies = []
    for tile in range(tiles):
        first = pl.multiple_of((2 * tile + parity) * columns, columns)
        copies.append(pltpu.make_async_copy(act_hbm.at[:, pl.ds(first, columns)], act.at[tile], sems.at[tile]))
        copies[-1].start(priority=1)

    def run():
        for tile in range(tiles):
            copies[tile].wait()
            product = jnp.dot(turned[...], act[tile], preferred_element_type=F32)
            for part in range(columns // width):
                piece = tile * (columns // width) + part
                block = product[:, part * width : (part + 1) * width]
                send_ref[piece] = block[:half].astype(BF16)
                keep_ref[piece] = block[half:]

    return run


def leading_kernel(
    core_ref, parity_ref, grads_hbm, left_hbm, right_hbm, act_hbm, send_ref, keep_ref, turned, half_ref, grads, left, act, sems, own
):
    core, parity = core_ref[0], parity_ref[0]
    half = send_ref.shape[1]
    copies = [
        pltpu.make_async_copy(grads_hbm, grads, own.at[0]),
        pltpu.make_async_copy(left_hbm, left, own.at[1]),
    ]
    for copy in copies:
        copy.start()
    run = products(1 - parity, act_hbm, act, turned, send_ref, keep_ref, sems)
    narrow = half_ref.shape[1]
    source = right_hbm.at[:, pl.ds(pl.multiple_of(core * narrow, narrow), narrow)]
    last = pltpu.make_async_copy(source, half_ref, own.at[2])
    last.start()
    for copy in copies:
        copy.wait()
    for part in range(2):
        first = pl.multiple_of((core ^ (1 - part)) * half, half)
        turned[part * half : (part + 1) * half] = lax.dot_general(
            left[pl.ds(first, half)],
            grads[...],
            (((1,), (1,)), ((), ())),
            preferred_element_type=F32,
        ).astype(BF16)
    run()
    last.wait()


def trailing_kernel(parity_ref, turned, act_hbm, send_ref, keep_ref, act, sems):
    products(parity_ref[0], act_hbm, act, turned, send_ref, keep_ref, sems)()


def sizes(shape, activations, out_grads):
    y_n, x_n, c_n, _ = shape
    tokens, features = activations.shape
    rows = out_grads.shape[1]
    tiles = y_n // 2
    blocks = (tiles * x_n, rows // c_n, features // (y_n * x_n))
    cost = pl.CostEstimate(
        flops=rows * tokens * features, bytes_accessed=tokens * features, transcendentals=0
    )
    return blocks, (tiles, tokens, features // y_n), cost


def leading(shape, at, activations, out_grads, input_inverse, output_inverse):
    blocks, tiles, cost = sizes(shape, activations, out_grads)
    hbm = pl.BlockSpec(memory_space=pl.ANY)
    operands = out_grads, output_inverse, input_inverse, activations
    operands = [pltpu.with_memory_space_constraint(a, pltpu.HBM) for a in operands]
    half = (input_inverse.shape[0], input_inverse.shape[1] // 2)
    return pl.pallas_call(
        leading_kernel,
        out_shape=(
            pltpu.VMEM(blocks, BF16),
            pltpu.VMEM(blocks, F32),
            pltpu.VMEM(out_grads.shape[::-1], BF16),
            pltpu.VMEM(half, BF16),
        ),
        in_specs=[SMEM, SMEM, hbm, hbm, hbm, hbm],
        out_specs=(VMEM, VMEM, VMEM, VMEM),
        scratch_shapes=[
            pltpu.VMEM(out_grads.shape, BF16),
            pltpu.VMEM(output_inverse.shape, BF16),
            pltpu.VMEM(tiles, BF16),
            pltpu.SemaphoreType.DMA((tiles[0],)),
            pltpu.SemaphoreType.DMA((3,)),
        ],
        compiler_params=pltpu.CompilerParams(vmem_limit_bytes=12 * 2**20),
        cost_estimate=cost,
    )(*at, *operands)


def trailing(shape, at, activations, out_grads, turned):
    blocks, tiles, cost = sizes(shape, activations, out_grads)
    return pl.pallas_call(
        trailing_kernel,
        out_shape=(pltpu.VMEM(blocks, BF16), pltpu.VMEM(blocks, F32)),
        in_specs=[SMEM, VMEM, pl.BlockSpec(memory_space=pl.ANY)],
        out_specs=(VMEM, VMEM),
        scratch_shapes=[
            pltpu.VMEM(tiles, BF16),
            pltpu.SemaphoreType.DMA((tiles[0],)),
        ],
        compiler_params=pltpu.CompilerParams(vmem_limit_bytes=12 * 2**20),
        cost_estimate=cost,
    )(at[1], turned, pltpu.with_memory_space_constraint(activations, pltpu.HBM))


def first_kernel(keep_ref, got_ref, send_ref):
    for block in range(send_ref.shape[0]):
        send_ref[block] = (keep_ref[block] + got_ref[block].astype(F32)).astype(BF16)


def first_sum(keep, got):
    return pl.pallas_call(
        first_kernel,
        out_shape=pltpu.VMEM(got.shape, BF16),
        in_specs=[VMEM, VMEM],
        out_specs=VMEM,
        compiler_params=pltpu.CompilerParams(vmem_limit_bytes=8 * 2**20),
    )(keep, got)


def second_kernel(keep_ref, more_ref, got_ref, total_hbm, total_ref, sems):
    copies = []
    for block in range(keep_ref.shape[0]):
        total = keep_ref[block] + got_ref[block].astype(F32) + more_ref[block].astype(F32)
        total_ref[block] = total.astype(BF16)
        copies.append(pltpu.make_async_copy(total_ref.at[block], total_hbm.at[block], sems.at[block]))
        copies[-1].start(priority=block % 2)
    for copy in copies:
        copy.wait()


def second_sum(keep, more, got):
    return pl.pallas_call(
        second_kernel,
        out_shape=pltpu.HBM(got.shape, BF16),
        in_specs=[VMEM, VMEM, VMEM],
        out_specs=pl.BlockSpec(memory_space=pl.ANY),
        scratch_shapes=[pltpu.VMEM(got.shape, BF16), pltpu.SemaphoreType.DMA((got.shape[0],))],
        compiler_params=pltpu.CompilerParams(vmem_limit_bytes=8 * 2**20),
    )(keep, more, got)


def sum_kernel(pieces_ref, _, total_ref):
    total = pieces_ref[0].astype(F32)
    for piece in range(1, pieces_ref.shape[0]):
        total += pieces_ref[piece].astype(F32)
    total_ref[...] = total.astype(BF16)


def sum_pieces(pieces, held):
    return pl.pallas_call(
        sum_kernel,
        out_shape=jax.ShapeDtypeStruct(pieces.shape[1:], BF16),
        in_specs=[VMEM, VMEM],
        out_specs=VMEM,
        compiler_params=pltpu.CompilerParams(vmem_limit_bytes=8 * 2**20),
    )(pieces, held)


def own_kernel(own_ref, near_ref, far_ref, out_ref):
    block = near_ref[...] + far_ref[...]
    out_ref[...] = jnp.dot(own_ref[...], block, preferred_element_type=F32).astype(BF16)


def own_right(own, near, far):
    return pl.pallas_call(
        own_kernel,
        out_shape=jax.ShapeDtypeStruct((own.shape[0], near.shape[1]), BF16),
        in_specs=[VMEM, VMEM, VMEM],
        out_specs=VMEM,
        compiler_params=pltpu.CompilerParams(vmem_limit_bytes=8 * 2**20),
    )(own, near, far)


def right_kernel(core_ref, done_ref, other_ref, near_ref, far_ref, out_ref):
    half = done_ref.shape[0]
    core = core_ref[0]
    out_ref[pl.ds(pl.multiple_of(core * half, half), half)] = done_ref[...]
    block = near_ref[...] + far_ref[...]
    first = pl.multiple_of((1 - core) * half, half)
    out_ref[pl.ds(first, half)] = jnp.dot(
        other_ref[...], block, preferred_element_type=F32
    ).astype(BF16)


def right(core, own, other, near, far):
    half, width = own.shape
    return pl.pallas_call(
        right_kernel,
        out_shape=jax.ShapeDtypeStruct((2 * half, width // 2), BF16),
        in_specs=[SMEM, VMEM, VMEM, VMEM, VMEM],
        out_specs=VMEM,
        compiler_params=pltpu.CompilerParams(vmem_limit_bytes=8 * 2**20),
    )(core.reshape(1), own_right(own, near, far), other, near, far)


def hold_kernel(block_ref, out_ref):
    rows = 16 if len(out_ref.shape) == 2 else 1
    out_ref[:rows] = block_ref[:rows]


def hold(block, flops):
    return pl.pallas_call(
        hold_kernel,
        out_shape=jax.ShapeDtypeStruct(block.shape, BF16),
        in_specs=[VMEM],
        out_specs=VMEM,
        input_output_aliases={0: 0},
        compiler_params=pltpu.CompilerParams(vmem_limit_bytes=4 * 2**20),
        cost_estimate=pl.CostEstimate(flops=flops, bytes_accessed=2**17, transcendentals=0),
    )(block)


def per_device(shape, activations, out_grads, input_inverse, output_inverse):
    core, parity = lax.axis_index("core"), lax.axis_index("yp")
    y_n = shape[0]

    def to_core(a):
        return lax.ppermute(a, AXES, pairs(shape, lambda y, x, c, m: (y, x, 1 - c, m)))

    def to_y(a):
        def move(y, x, c, m):
            return (((y + c) % y_n ^ 1) - c) % y_n, x, c, m

        return lax.ppermute(a, AXES, pairs(shape, move))

    at = core.reshape(1), parity.reshape(1)
    send, keep, turned, half = leading(shape, at, activations, out_grads, input_inverse, output_inverse)
    lower, higher = spread(shape)
    near = lax.ppermute(half, AXES, lower)
    send_y, turned = lax.optimization_barrier((first_sum(keep, to_core(send)), turned))
    send, rest = trailing(shape, at, activations, out_grads, turned)
    got_y = hold(to_y(send_y), 5 * 10**9)
    total = second_sum(rest, got_y, to_core(send))
    total, half = lax.optimization_barrier((total, half))
    far = lax.ppermute(half, AXES, higher)
    pieces = lax.all_to_all(total, ("yk", "xh"), 0, 0)
    near = hold(near, 5 * 10**10)
    gathered = sum_pieces(pieces, near)
    return right(core, gathered, to_core(gathered), near, far)


def solution(mesh):
    dp_count, mp_count = mesh.devices.shape
    shape = (dp_count // 4, 2, 2, mp_count)
    split = Mesh(mesh.devices.reshape(shape[0] // 2, 2, *shape[1:]), AXES)
    dp = AXES[:4]
    in_specs = (P(dp, None), P(dp, "mp"), P("mp", None), P("mp", None))
    return jax.shard_map(
        functools.partial(per_device, shape),
        mesh=split,
        in_specs=in_specs,
        out_specs=P("mp", dp),
        check_vma=False,
    )
```
